128 devices in a mesh: src: 16 (over z, y), tgt: 8 (over x, core).
Axes of the slice: x: 4, y: 4, z: 4, core: 2. Of those that a mesh axis runs over, the one named last changes fastest.
Arguments:
- src_points: float32 [64, 32768], P(None, ('src', 'tgt')), as said below
- tgt_points: float32 [64, 32768], P(None, ('tgt', 'src')), as said below
- log_a: float32 [32768], P('src'), may hold values from -1 to 1
- log_b: float32 [32768], P('tgt'), may hold values from -1 to 1
- g_init: float32 [32768], P('tgt')
Outputs:
- f_out: float32 [32768], P('src')
- g_out: float32 [32768], P('tgt')
- grad_src: float32 [64, 32768], P(None, ('src', 'tgt'))
- grad_tgt: float32 [64, 32768], P(None, ('tgt', 'src'))
The draws below stay inside these ranges and needn't reach their ends.
Inputs may be any that keep to these rules, and one draw needn't show every extreme that they name: `src_points`: entries of order one or less. `tgt_points`: entries of order one or less.
All inputs are finite; a program needn't handle non-finite values.
Results may differ from the reference program's by a relative error of at most 0.0003.
Values sent between devices are 32-bit elements; how exact they have to be, the bound alone decides.
A program may use at most 64 MiB of HBM per device.

```python
import math
import jax
import jax.numpy as jnp
from jax import lax

D = 64
SRC_DEV = 2048
NS = 32768
NT = 32768


def make_points(key, count, salt, low, high):
    first, second = jax.random.split(jax.random.fold_in(key, salt))
    base = jax.random.normal(first, (D, count), jnp.float32)
    scales = jnp.exp(jax.random.uniform(second, (1, count), jnp.float32, minval=low, maxval=high))
    return base * scales


def draw_src_points(key, part):
    sources = make_points(key, NS, 11, math.log(0.25), math.log(0.25))
    return sources


def draw_tgt_points(key, part):
    targets = make_points(key, NT, 12, math.log(0.25), math.log(0.25))
    return targets


def draw_g_init(key, part):
    key = jax.random.fold_in(key, 5)
    values = jax.random.normal(key, (NT,), jnp.float32)
    return values


def block_scale(stream_key, shape, shards, smallest, largest):
    def one(position, parts):
        heights = jax.random.uniform(jax.random.fold_in(jax.random.fold_in(stream_key, 6), position), (parts,), jnp.float32, smallest / len(shards), largest / len(shards))
        return jnp.repeat(jnp.exp(heights), shape[position] // parts).reshape((-1,) + (1,) * (len(shape) - position - 1))

    loudness = one(*shards[0])
    for cut in shards[1:]:
        loudness = loudness * one(*cut)
    return loudness


def setup_inputs(seed: int = 0) -> dict:
    arg_keys = jax.random.split(jax.random.key(seed), 6)
    src_points = draw_src_points(jax.random.fold_in(arg_keys[5], 71), 0)
    tgt_points = draw_tgt_points(jax.random.fold_in(arg_keys[5], 71), 0)
    log_a = jnp.clip(jax.random.uniform(arg_keys[2], (NS,), jnp.float32, -1.0, 1.0) * block_scale(arg_keys[2], (NS,), ((0, 16),), -0.4, 0.0), -1.0, 1.0)
    log_b = jnp.clip(jax.random.uniform(arg_keys[3], (NT,), jnp.float32, -1.0, 1.0) * block_scale(arg_keys[3], (NT,), ((0, 8),), -0.4, 0.0), -1.0, 1.0)
    g_init = draw_g_init(jax.random.fold_in(arg_keys[5], 71), 0)
    return {"src_points": src_points, "tgt_points": tgt_points, "log_a": log_a, "log_b": log_b, "g_init": g_init}


epsilon = 0.5
tile_rows = 512
highest = lax.Precision.HIGHEST


def cost_tile(src_part, targets, tgt_square):
    cross = lax.dot_general(src_part, targets, (((0,), (0,)), ((), ())), precision=highest, preferred_element_type=jnp.float32)
    return jnp.sum(src_part * src_part, axis=0)[:, None] + tgt_square[None, :] - 2.0 * cross


def reference(src_points, tgt_points, log_a, log_b, g_init):
    row_block = min(tile_rows, SRC_DEV)
    num_blocks = NS // row_block
    tgt_square = jnp.sum(tgt_points * tgt_points, axis=0)
    src_tiles = src_points.reshape(D, num_blocks, row_block).transpose(1, 0, 2)
    weight_tiles = log_a.reshape(num_blocks, row_block)

    def row_half(pieces):
        src_part, weights = pieces
        scores = (g_init[None, :] - cost_tile(src_part, tgt_points, tgt_square)) / epsilon
        peak = jnp.max(scores, axis=1)
        total = jnp.sum(jnp.exp(scores - peak[:, None]), axis=1)
        return epsilon * (weights - (peak + jnp.log(total)))

    row_pot = lax.map(row_half, (src_tiles, weight_tiles))
    f_out = row_pot.reshape(NS)

    def column_peak(pieces):
        src_part, row_part = pieces
        scores = (row_part[:, None] - cost_tile(src_part, tgt_points, tgt_square)) / epsilon
        return jnp.max(scores, axis=0)

    peak = jnp.max(lax.map(column_peak, (src_tiles, row_pot)), axis=0)

    def column_total(total, pieces):
        src_part, row_part = pieces
        scores = (row_part[:, None] - cost_tile(src_part, tgt_points, tgt_square)) / epsilon
        return total + jnp.sum(jnp.exp(scores - peak[None, :]), axis=0), None

    total, unused = lax.scan(column_total, jnp.zeros((NT,), jnp.float32), (src_tiles, row_pot))
    g_out = epsilon * (log_b - (peak + jnp.log(total)))

    def gradient_step(state, pieces):
        col_mass, pulled = state
        src_part, row_part = pieces
        cost = cost_tile(src_part, tgt_points, tgt_square)
        plan = jnp.exp((row_part[:, None] + g_out[None, :] - cost) / epsilon)
        row_mass = jnp.sum(plan, axis=1)
        pushed = lax.dot_general(tgt_points, plan, (((1,), (1,)), ((), ())), precision=highest, preferred_element_type=jnp.float32)
        src_grad = 2.0 * (src_part * row_mass[None, :] - pushed)
        col_mass = col_mass + jnp.sum(plan, axis=0)
        pulled = pulled + jnp.dot(src_part, plan, precision=highest, preferred_element_type=jnp.float32)
        return (col_mass, pulled), src_grad

    start_state = (jnp.zeros((NT,), jnp.float32), jnp.zeros((D, NT), jnp.float32))
    (col_mass, pulled), src_grads = lax.scan(gradient_step, start_state, (src_tiles, row_pot))
    grad_src = src_grads.transpose(1, 0, 2).reshape(D, NS)
    grad_tgt = 2.0 * (tgt_points * col_mass[None, :] - pulled)
    return f_out, g_out, grad_src, grad_tgt
```

```python
import functools

import jax
import jax.numpy as jnp
from jax import lax
from jax.experimental import pallas as pl
from jax.experimental.pallas import tpu as pltpu
from jax.sharding import PartitionSpec as P

epsilon = 0.5
LOG2E = 1.4426950408889634
LN2 = 0.6931471805599453
SCALE = LOG2E / epsilon
LO_SCALE = 2.0**17
PT_SCALE = 2.0**4
F8_MAX = 448.0
MESH = pl.DeviceIdType.MESH
f32, bf16, f8 = jnp.float32, jnp.bfloat16, jnp.float8_e4m3fn
LANES = 128


def split(value):
    high = value.astype(bf16).astype(f32)
    return high, value - high


def to_f8(value):
    return jnp.clip(value, -F8_MAX, F8_MAX).astype(f8)


def wide(column, times):
    return jnp.concatenate([column] * times, axis=1)


def kernel(
    ns, ny, nt, nc, comm,
    src_ref, tgt_ref, la_ref, lb_ref, g_ref,
    f_ref, go_ref, gs_ref, gt_ref,
    xall, yslots, xs, yt, w, w8, bcol, sbuf, mrun, lrun, arow, mcol, rowstat, colstat, srow,
    ehi, elo, pulled, left, left8, gsend, gsrecv, gtrecv,
    sx, rx, sy, ry, sr, rr, sc, rc, sgs, rgs, sgt, rgt,
):
    blk = src_ref.shape[1]
    width = src_ref.shape[0]
    rows, cols = nt * blk, ns * blk
    if comm:
        p, q = lax.axis_index("src"), lax.axis_index("tgt")
    else:
        p, q = jnp.int32(0), jnp.int32(0)

    def shifted(at, step, count, minor, sign):
        major = count // minor
        a = lax.rem(at // minor + sign * (step // minor) + major, major)
        b = lax.rem(lax.rem(at, minor) + sign * lax.rem(step, minor) + minor, minor)
        return a * minor + b

    def src_peer(step, sign):
        return shifted(p, jnp.int32(step), ns, ny, sign)

    def tgt_peer(step, sign):
        return shifted(q, jnp.int32(step), nt, nc, sign)

    def lanes(owner):
        return pl.ds(pl.multiple_of(owner * blk, blk), blk)

    def remote(source, target, send, recv, device):
        return pltpu.make_async_remote_copy(
            src_ref=source, dst_ref=target, send_sem=send, recv_sem=recv, device_id=device, device_id_type=MESH
        )

    tsteps = range(1, nt) if comm else ()
    ssteps = range(1, ns) if comm else ()

    def x_copy(k, owner, to):
        return remote(src_ref, xall.at[:, lanes(owner)], sx.at[k], rx.at[k], (p, to))

    def y_copy(k):
        return remote(tgt_ref, yslots.at[k], sy.at[k], ry.at[k], (src_peer(k, 1), q))

    def r_copy(k, owner, to):
        return remote(rowstat.at[q], rowstat.at[owner], sr.at[k], rr.at[k], (p, to))

    def c_copy(k, owner, to):
        return remote(colstat.at[p], colstat.at[owner], sc.at[k], rc.at[k], (to, q))

    def gs_copy(k):
        return remote(gsend.at[k], gsrecv.at[k], sgs.at[k], rgs.at[k], (p, tgt_peer(k, -1)))

    def gt_copy(k):
        return remote(pulled.at[k], gtrecv.at[k], sgt.at[k], rgt.at[k], (src_peer(k, -1), q))

    if comm:
        barrier = pltpu.get_barrier_semaphore()
        for k in tsteps:
            pl.semaphore_signal(barrier, inc=1, device_id=(p, tgt_peer(k, 1)), device_id_type=MESH)
        for k in ssteps:
            pl.semaphore_signal(barrier, inc=1, device_id=(src_peer(k, 1), q), device_id_type=MESH)
        pl.semaphore_wait(barrier, nt - 1 + ns - 1)

    for k in tsteps:
        x_copy(k, q, tgt_peer(k, 1)).start()
    for k in ssteps:
        y_copy(k).start()
    xall[:, lanes(q)] = src_ref[...]
    yslots[0] = tgt_ref[...]

    def prepare_targets(k, slot):
        y = yslots[k]
        scaled = y * (2.0 * SCALE)
        parts = jnp.concatenate(split(scaled), axis=0).T.astype(bf16)
        at = pl.ds(pl.multiple_of(k * blk, blk), blk)
        yt[at, 0:LANES] = parts
        yt[at, LANES : 2 * LANES] = parts
        bias = SCALE * (g_ref[:, lanes(src_peer(k, -1))] - jnp.sum(y * y, axis=0, keepdims=True))
        bcol[slot] = jnp.broadcast_to(bias, (LANES, blk)).T

    def prepare_sources(j):
        at = pl.ds(j * blk, blk)
        x = xall[:, at]
        high, low = split(x)
        xs[0:width, at] = high.astype(bf16)
        xs[width : 2 * width, at] = high.astype(bf16)
        xs[2 * width : 3 * width, at] = low.astype(bf16)
        xs[3 * width : 4 * width, at] = low.astype(bf16)
        w[at, 0:LANES] = jnp.concatenate([high, low], axis=0).T.astype(bf16)
        w[at, LANES : 2 * LANES] = jnp.ones((blk, LANES), bf16)
        parts = jnp.concatenate([x * PT_SCALE, jnp.ones_like(x)], axis=0).T
        w8[at, :] = to_f8(parts)

    def scores(k, slot):
        at = pl.ds(pl.multiple_of(k * blk, blk), blk)
        sbuf[slot] = jnp.dot(yt[at, :], xs[...], preferred_element_type=f32)

    def wait_y(k):
        if comm:
            y_copy(k).wait_recv()

    prepare_targets(0, 0)
    for k in tsteps:
        x_copy(k, tgt_peer(k, -1), tgt_peer(k, 1)).wait_recv()
    for j in range(nt):
        prepare_sources(j)

    mrun[...] = jnp.full(mrun.shape, -jnp.inf, f32)
    lrun[...] = jnp.zeros(lrun.shape, f32)
    chunk = min(512, rows)

    def row_pass(slot):
        for c in range(rows // chunk):
            at = slice(c * chunk, (c + 1) * chunk)
            old = mrun[:, at]
            top = old
            for r in range(blk // 8):
                rs = slice(8 * r, 8 * r + 8)
                top = jnp.maximum(top, sbuf[slot, rs, at] + wide(bcol[slot, rs, :], chunk // LANES))
            total = lrun[:, at] * jnp.exp2(old - top)
            for r in range(blk // 8):
                rs = slice(8 * r, 8 * r + 8)
                total = total + jnp.exp2(sbuf[slot, rs, at] + (wide(bcol[slot, rs, :], chunk // LANES) - top))
            mrun[:, at] = top
            lrun[:, at] = total

    scores(0, 0)

    def row_steps(pair, carry):
        for slot in range(2):
            k = 2 * pair + slot + 1
            wait_y(k)
            prepare_targets(k, 1 - slot)
            scores(k, 1 - slot)
            row_pass(slot)
        return carry

    lax.fori_loop(0, ns // 2 - 1, row_steps, 0)
    wait_y(ns - 1)
    prepare_targets(ns - 1, 1)
    scores(ns - 1, 1)
    row_pass(0)
    row_pass(1)

    top = jnp.max(mrun[...], axis=0, keepdims=True)
    rowstat[q, 0:1, :] = top
    rowstat[q, 1:2, :] = jnp.sum(lrun[...] * jnp.exp2(mrun[...] - top), axis=0, keepdims=True)
    for k in tsteps:
        r_copy(k, q, tgt_peer(k, 1)).start()
    scores(0, 0)
    for k in tsteps:
        r_copy(k, tgt_peer(k, -1), tgt_peer(k, 1)).wait_recv()
    top = rowstat[0, 0:1, :]
    for j in range(1, nt):
        top = jnp.maximum(top, rowstat[j, 0:1, :])
    total = jnp.zeros_like(top)
    for j in range(nt):
        total = total + rowstat[j, 1:2, :] * jnp.exp2(rowstat[j, 0:1, :] - top)
    lse = top + jnp.log(total) * LOG2E
    arow[...] = jnp.broadcast_to(LOG2E * la_ref[...] - lse, arow.shape)
    x = xall[...]
    f_ref[...] = epsilon * la_ref[...] - (epsilon * LN2) * lse + jnp.sum(x * x, axis=0, keepdims=True)

    def expos(k, slot):
        tops = sbuf[slot, :, 0:LANES] + arow[0:1, 0:LANES]
        for c in range(1, rows // LANES):
            at = slice(c * LANES, (c + 1) * LANES)
            tops = jnp.maximum(tops, sbuf[slot, :, at] + arow[0:1, at])
        mcol[...] = jnp.broadcast_to(jnp.max(tops, axis=1, keepdims=True), mcol.shape)
        for r in range(blk // 32):
            rs = slice(32 * r, 32 * r + 32)
            to = pl.ds(pl.multiple_of(k * blk + 32 * r, 32), 32)
            for c in range(rows // chunk):
                at = slice(c * chunk, (c + 1) * chunk)
                e = jnp.exp2(sbuf[slot, rs, at] + (arow[0:1, at] - wide(mcol[rs, :], chunk // LANES)))
                high = e.astype(bf16)
                ehi[to, at] = high
                elo[to, at] = ((e - high.astype(f32)) * LO_SCALE).astype(f8)

    def pull(k):
        at = pl.ds(pl.multiple_of(k * blk, blk), blk)
        main = jnp.dot(ehi[at, :], w[...], preferred_element_type=f32)
        rest = jnp.dot(elo[at, :], w8[...], preferred_element_type=f32)
        first = lax.broadcasted_iota(jnp.int32, (blk, LANES), 1) == 0
        sums = main[:, 0:LANES].T
        rest = rest.T
        stats = jnp.where(first, mcol[...], main[:, LANES : 2 * LANES]).T
        pulled[k] = sums[0:width] + sums[width : 2 * width] + rest[0:width] * (1.0 / (LO_SCALE * PT_SCALE))
        owner = lanes(src_peer(k, -1))
        colstat[p, 0:1, owner] = stats[0:1, :]
        colstat[p, 1:2, owner] = stats[1:2, :] + rest[width : width + 1, :] * (1.0 / LO_SCALE)

    def col_steps(pair, carry):
        for slot in range(2):
            k = 2 * pair + slot
            scores(k + 1, 1 - slot)
            expos(k, slot)
            pull(k)
        return carry

    lax.fori_loop(0, ns // 2 - 1, col_steps, 0)
    scores(ns - 1, 1)
    expos(ns - 2, 0)
    pull(ns - 2)
    expos(ns - 1, 1)
    pull(ns - 1)

    for k in ssteps:
        c_copy(k, p, src_peer(k, 1)).start()
    for k in ssteps:
        c_copy(k, src_peer(k, -1), src_peer(k, 1)).wait_recv()
    top = colstat[0, 0:1, :]
    for j in range(1, ns):
        top = jnp.maximum(top, colstat[j, 0:1, :])
    total = jnp.zeros_like(top)
    for j in range(ns):
        total = total + colstat[j, 1:2, :] * jnp.exp2(colstat[j, 0:1, :] - top)
    lse = top + jnp.log(total) * LOG2E
    srow[0:1, :] = jnp.exp2(LOG2E * lb_ref[...] + (colstat[p, 0:1, :] - lse))
    go_ref[...] = epsilon * lb_ref[...] - (epsilon * LN2) * lse

    def weigh(k, carry):
        owner = lanes(src_peer(k, -1))
        at = pl.ds(pl.multiple_of(k * blk, blk), blk)
        s = srow[0:1, owner]
        y = yslots[k]
        go_ref[:, owner] = go_ref[:, owner] + jnp.sum(y * y, axis=0, keepdims=True)
        pulled[k] = pulled[k] * s
        ys = y * s
        high, low = split(ys)
        shigh, slow = split(jnp.broadcast_to(s, (8, blk)))
        left[:, at] = jnp.concatenate([high, low, shigh, slow], axis=0).astype(bf16)
        left8[:, at] = to_f8(jnp.concatenate([ys, jnp.broadcast_to(s, (32, blk))], axis=0) * PT_SCALE)
        if comm:

            @pl.when(k > 0)
            def _():
                gt_copy(k).start()

        return carry

    lax.fori_loop(0, ns, weigh, 0)

    def push(k):
        at = lanes(tgt_peer(k, -1))
        main = jnp.dot(left[...], ehi[:, at], preferred_element_type=f32)
        rest = jnp.dot(left8[...], elo[:, at], preferred_element_type=f32) * (1.0 / (LO_SCALE * PT_SCALE))
        moved = main[0:width] + main[width : 2 * width] + rest[0:width]
        mass = main[2 * width : 2 * width + 1] + main[2 * width + 8 : 2 * width + 9] + rest[width : width + 1]
        return 2.0 * (xall[:, at] * mass - moved)

    def push_step(k, carry):
        gsend[k] = push(k)
        if comm:
            gs_copy(k).start()
        return carry

    lax.fori_loop(1, nt, push_step, 0)
    grad = push(0)

    mine = lanes(p)
    moved = pulled[0]
    for k in range(1, ns):
        if comm:
            gt_copy(k).wait_recv()
        moved = moved + gtrecv[k]
    gt_ref[...] = 2.0 * (tgt_ref[...] * jnp.exp2(LOG2E * lb_ref[:, mine]) - moved)
    for k in range(1, nt):
        if comm:
            gs_copy(k).wait_recv()
        grad = grad + gsrecv[k]
    gs_ref[...] = grad

    for k in tsteps:
        x_copy(k, q, tgt_peer(k, 1)).wait_send()
        r_copy(k, q, tgt_peer(k, 1)).wait_send()
        gs_copy(k).wait_send()
    for k in ssteps:
        y_copy(k).wait_send()
        c_copy(k, p, src_peer(k, 1)).wait_send()
        gt_copy(k).wait_send()


def call(ns, ny, nt, nc, comm, width, blk):
    rows, cols = nt * blk, ns * blk
    vmem = pl.BlockSpec(memory_space=pltpu.VMEM)
    dma = pltpu.SemaphoreType.DMA
    scratch = [
        ((width, rows), f32), ((ns, width, blk), f32), ((4 * width, rows), bf16), ((cols, 2 * LANES), bf16),
        ((rows, 2 * LANES), bf16), ((rows, LANES), f8), ((2, blk, LANES), f32), ((2, blk, rows), f32),
        ((8, rows), f32), ((8, rows), f32), ((8, rows), f32), ((blk, LANES), f32),
        ((nt, 2, rows), f32), ((ns, 2, cols), f32), ((8, cols), f32),
        ((cols, rows), bf16), ((cols, rows), f8), ((ns, width, blk), f32),
        ((2 * width + 16, cols), bf16), ((width + 32, cols), f8),
        ((nt, width, blk), f32), ((nt, width, blk), f32), ((ns, width, blk), f32),
    ]
    sems = [nt, nt, ns, ns, nt, nt, ns, ns, nt, nt, ns, ns]
    params = dict(vmem_limit_bytes=60 * 2**20, has_side_effects=True)
    if comm:
        params["collective_id"] = 0
    return pl.pallas_call(
        functools.partial(kernel, ns, ny, nt, nc, comm),
        out_shape=[
            jax.ShapeDtypeStruct((1, rows), f32),
            jax.ShapeDtypeStruct((1, cols), f32),
            jax.ShapeDtypeStruct((width, blk), f32),
            jax.ShapeDtypeStruct((width, blk), f32),
        ],
        in_specs=[vmem] * 5,
        out_specs=[vmem] * 4,
        scratch_shapes=[pltpu.VMEM(*s) for s in scratch] + [dma((n,)) for n in sems],
        compiler_params=pltpu.CompilerParams(**params),
        name="sinkhorn",
    )


def solution(mesh):
    ns, nt = mesh.shape["src"], mesh.shape["tgt"]
    ny = 4 if ns % 4 == 0 else 1
    nc = 2 if nt % 2 == 0 else 1

    def per_device(src_points, tgt_points, log_a, log_b, g_init):
        width, blk = src_points.shape
        run = call(ns, ny, nt, nc, True, width, blk)
        f, g, grad_src, grad_tgt = run(
            src_points, tgt_points, log_a.reshape(1, -1), log_b.reshape(1, -1), g_init.reshape(1, -1)
        )
        return f.reshape(-1), g.reshape(-1), grad_src, grad_tgt

    in_specs = (P(None, ("src", "tgt")), P(None, ("tgt", "src")), P("src"), P("tgt"), P("tgt"))
    out_specs = (P("src"), P("tgt"), P(None, ("src", "tgt")), P(None, ("tgt", "src")))
    return jax.shard_map(per_device, mesh=mesh, in_specs=in_specs, out_specs=out_specs, check_vma=False)
```

```python
import functools

import jax
import jax.numpy as jnp
from jax import lax
from jax.experimental import pallas as pl
from jax.experimental.pallas import tpu as pltpu
from jax.sharding import PartitionSpec as P

epsilon = 0.5
LOG2E = 1.4426950408889634
LN2 = 0.6931471805599453
SCALE = LOG2E / epsilon
LIFT = 17.0
PT_SCALE = 2.0**4
F8_MAX = 448.0
MESH = pl.DeviceIdType.MESH
f32, bf16, f8 = jnp.float32, jnp.bfloat16, jnp.float8_e4m3fn
LANES = 128


def split(value):
    high = value.astype(bf16).astype(f32)
    return high, value - high


def to_f8(value):
    return jnp.clip(value, -F8_MAX, F8_MAX).astype(f8)


def wide(column, times):
    return jnp.concatenate([column] * times, axis=1)


def column_parts(ns):
    cuts = [0, 6, 12, 16] if ns == 16 else [0, ns // 2, ns]
    return list(zip(cuts[:-1], cuts[1:]))


def kernel(
    ns, ny, nt, nc, comm,
    src_ref, tgt_ref, la_ref, lb_ref, g_ref,
    f_ref, go_ref, gs_ref, gt_ref,
    xall, yslots, xs, yt, w, w8, bcol, table, mrun, lrun, arow, mcol, rowstat, colstat, srow,
    ehi, elo, pulled, left, left8, acc, gsend, gsrecv, gtrecv,
    sx, rx, sy, ry, sr, rr, sc, rc, sgs, rgs, sgt, rgt,
):
    blk = src_ref.shape[1]
    width = src_ref.shape[0]
    rows, cols = nt * blk, ns * blk
    parts = column_parts(ns)
    if comm:
        p, q = lax.axis_index("src"), lax.axis_index("tgt")
    else:
        p, q = jnp.int32(0), jnp.int32(0)

    def shifted(at, step, count, minor, sign):
        major = count // minor
        a = lax.rem(at // minor + sign * (step // minor) + major, major)
        b = lax.rem(lax.rem(at, minor) + sign * lax.rem(step, minor) + minor, minor)
        return a * minor + b

    def src_peer(step, sign):
        return shifted(p, jnp.int32(step), ns, ny, sign)

    def tgt_peer(step, sign):
        return shifted(q, jnp.int32(step), nt, nc, sign)

    def place(b):
        major = ns // ny
        return lax.rem(p // ny - b // ny + major, major) * ny + lax.rem(lax.rem(p, ny) - b % ny + ny, ny)

    def lanes(owner):
        return pl.ds(pl.multiple_of(owner * blk, blk), blk)

    def remote(source, target, send, recv, device):
        return pltpu.make_async_remote_copy(
            src_ref=source, dst_ref=target, send_sem=send, recv_sem=recv, device_id=device, device_id_type=MESH
        )

    tsteps = range(1, nt) if comm else ()
    ssteps = range(1, ns) if comm else ()

    def x_copy(k, owner, to):
        return remote(src_ref, xall.at[:, lanes(owner)], sx.at[k], rx.at[k], (p, to))

    def y_copy(k):
        return remote(tgt_ref, yslots.at[k], sy.at[k], ry.at[k], (src_peer(k, 1), q))

    def r_copy(k, owner, to):
        return remote(rowstat.at[q], rowstat.at[owner], sr.at[k], rr.at[k], (p, to))

    def c_copy(part, k, owner, to):
        at = pl.ds(parts[part][0] * blk, (parts[part][1] - parts[part][0]) * blk)
        sem = part * ns + k
        return remote(colstat.at[p, :, at], colstat.at[owner, :, at], sc.at[sem], rc.at[sem], (to, q))

    def gs_copy(k):
        return remote(gsend.at[k], gsrecv.at[k], sgs.at[k], rgs.at[k], (p, tgt_peer(k, -1)))

    def gt_copy(b):
        return remote(pulled.at[b], gtrecv.at[p], sgt.at[b], rgt.at[p], (b, q))

    def gt_arrival(k):
        owner = src_peer(k, -1)
        return remote(pulled.at[owner], gtrecv.at[owner], sgt.at[owner], rgt.at[owner], (owner, q))

    if comm:
        barrier = pltpu.get_barrier_semaphore()
        for k in tsteps:
            pl.semaphore_signal(barrier, inc=1, device_id=(p, tgt_peer(k, 1)), device_id_type=MESH)
        for k in ssteps:
            pl.semaphore_signal(barrier, inc=1, device_id=(src_peer(k, 1), q), device_id_type=MESH)
        pl.semaphore_wait(barrier, nt - 1 + ns - 1)

    for k in tsteps:
        x_copy(k, q, tgt_peer(k, 1)).start()
    for k in ssteps:
        y_copy(k).start()
    xall[:, lanes(q)] = src_ref[...]
    yslots[0] = tgt_ref[...]

    def prepare_targets(k, slot):
        y = yslots[k]
        scaled = y * (2.0 * SCALE)
        parts = jnp.concatenate(split(scaled), axis=0).T.astype(bf16)
        at = pl.ds(pl.multiple_of(k * blk, blk), blk)
        yt[at, 0:LANES] = parts
        yt[at, LANES : 2 * LANES] = parts
        bias = SCALE * (g_ref[:, lanes(src_peer(k, -1))] - jnp.sum(y * y, axis=0, keepdims=True))
        bcol[slot] = jnp.broadcast_to(bias, (LANES, blk)).T

    def prepare_sources(j):
        at = pl.ds(j * blk, blk)
        x = xall[:, at]
        high, low = split(x)
        xs[0:width, at] = high.astype(bf16)
        xs[width : 2 * width, at] = high.astype(bf16)
        xs[2 * width : 3 * width, at] = low.astype(bf16)
        xs[3 * width : 4 * width, at] = low.astype(bf16)
        w[at, 0:LANES] = jnp.concatenate([high, low], axis=0).T.astype(bf16)
        w[at, LANES : 2 * LANES] = jnp.ones((blk, LANES), bf16)
        parts = jnp.concatenate([x * PT_SCALE, jnp.ones_like(x)], axis=0).T
        w8[at, :] = to_f8(parts)

    def scores(k):
        table[k] = jnp.dot(yt[k * blk : (k + 1) * blk, :], xs[...], preferred_element_type=f32)

    def wait_y(k):
        if comm:
            y_copy(k).wait_recv()

    prepare_targets(0, 0)
    for k in tsteps:
        x_copy(k, tgt_peer(k, -1), tgt_peer(k, 1)).wait_recv()
    for j in range(nt):
        prepare_sources(j)

    mrun[...] = jnp.full(mrun.shape, -jnp.inf, f32)
    lrun[...] = jnp.zeros(lrun.shape, f32)
    chunk = min(512, rows)

    def row_pass(k):
        slot = k % 2
        for c in range(rows // chunk):
            at = slice(c * chunk, (c + 1) * chunk)
            old = mrun[:, at]
            top = old
            for r in range(blk // 8):
                rs = slice(8 * r, 8 * r + 8)
                top = jnp.maximum(top, table[k, rs, at] + wide(bcol[slot, rs, :], chunk // LANES))
            total = lrun[:, at] * jnp.exp2(old - top)
            for r in range(blk // 8):
                rs = slice(8 * r, 8 * r + 8)
                total = total + jnp.exp2(table[k, rs, at] + (wide(bcol[slot, rs, :], chunk // LANES) - top))
            mrun[:, at] = top
            lrun[:, at] = total

    scores(0)
    for k in range(ns):
        if k + 1 < ns:
            wait_y(k + 1)
            prepare_targets(k + 1, (k + 1) % 2)
            scores(k + 1)
        row_pass(k)

    top = jnp.max(mrun[...], axis=0, keepdims=True)
    rowstat[q, 0:1, :] = top
    rowstat[q, 1:2, :] = jnp.sum(lrun[...] * jnp.exp2(mrun[...] - top), axis=0, keepdims=True)
    for k in tsteps:
        r_copy(k, q, tgt_peer(k, 1)).start()
    for k in tsteps:
        r_copy(k, tgt_peer(k, -1), tgt_peer(k, 1)).wait_recv()
    top = rowstat[0, 0:1, :]
    for j in range(1, nt):
        top = jnp.maximum(top, rowstat[j, 0:1, :])
    total = jnp.zeros_like(top)
    for j in range(nt):
        total = total + rowstat[j, 1:2, :] * jnp.exp2(rowstat[j, 0:1, :] - top)
    lse = top + jnp.log(total) * LOG2E
    arow[...] = jnp.broadcast_to(LOG2E * la_ref[...] - lse, arow.shape)
    x = xall[...]
    f_ref[...] = epsilon * la_ref[...] - (epsilon * LN2) * lse + jnp.sum(x * x, axis=0, keepdims=True)

    def keep(e, slot, rs, at):
        high = e.astype(bf16)
        rs = slice(slot * blk + rs.start, slot * blk + rs.stop)
        ehi[rs, at] = high
        elo[rs, at] = (e - high.astype(f32)).astype(f8)

    def tops(b, rs):
        k = place(b)
        top = None
        for c in range(rows // LANES):
            at = slice(c * LANES, (c + 1) * LANES)
            z = table[k, rs, at] + arow[0:1, at]
            table[k, rs, at] = z
            top = z if top is None else jnp.maximum(top, z)
        top = jnp.max(top, axis=1, keepdims=True) - LIFT
        mcol[b % 3, rs, :] = jnp.broadcast_to(top, (rs.stop - rs.start, LANES))

    def expos(b, rs):
        k = place(b)
        for r in range(rs.start, rs.stop, 32):
            part = slice(r, r + 32)
            shift = wide(mcol[b % 3, part, :], chunk // LANES)
            for c in range(rows // chunk):
                at = slice(c * chunk, (c + 1) * chunk)
                e = jnp.exp2(table[k, part, at] - shift)
                table[k, part, at] = e
                keep(e, b % 2, part, at)

    half = rows // 2

    def pull_product(b, piece):
        rs = slice((b % 2) * blk, (b % 2 + 1) * blk)
        at = slice(piece % 2 * half, (piece % 2 + 1) * half)
        if piece < 2:
            return jnp.dot(ehi[rs, at], w[at, :], preferred_element_type=f32)
        return jnp.dot(elo[rs, at], w8[at, :], preferred_element_type=f32)

    def pull_finish(b, products):
        main = products[0] + products[1]
        rest = (products[2] + products[3]).T
        first = lax.broadcasted_iota(jnp.int32, (blk, LANES), 1) == 0
        sums = main[:, 0:LANES].T
        stats = jnp.where(first, mcol[b % 3], main[:, LANES : 2 * LANES]).T
        pulled[b] = sums[0:width] + sums[width : 2 * width] + rest[0:width] * (1.0 / PT_SCALE)
        at = slice(b * blk, (b + 1) * blk)
        colstat[p, 0:1, at] = stats[0:1, :]
        colstat[p, 1:2, at] = stats[1:2, :] + rest[width : width + 1, :]
        if comm:

            @pl.when(p != b)
            def _():
                gt_copy(b).start()

        for part, (_, stop) in enumerate(parts):
            if b == stop - 1:
                for k in ssteps:
                    c_copy(part, k, p, src_peer(k, 1)).start()

    tops(0, slice(0, blk))
    for b in range(ns + 1):
        products = []
        for piece in range(4):
            rs = slice(piece * (blk // 4), (piece + 1) * (blk // 4))
            if b:
                products.append(pull_product(b - 1, piece))
            if b < ns:
                expos(b, rs)
            if b + 1 < ns:
                tops(b + 1, rs)
        if b:
            pull_finish(b - 1, products)

    def weigh(part):
        start, stop = parts[part]
        for k in ssteps:
            c_copy(part, k, src_peer(k, -1), src_peer(k, 1)).wait_recv()
        at = slice(start * blk, stop * blk)
        top = colstat[0, 0:1, at]
        for j in range(1, ns):
            top = jnp.maximum(top, colstat[j, 0:1, at])
        total = jnp.zeros_like(top)
        for j in range(ns):
            total = total + colstat[j, 1:2, at] * jnp.exp2(colstat[j, 0:1, at] - top)
        lse = top + jnp.log(total) * LOG2E
        weight = LOG2E * lb_ref[:, at] - lse
        srow[0:1, at] = weight
        go_ref[:, at] = epsilon * lb_ref[:, at] - (epsilon * LN2) * lse
        weight = jnp.exp2(weight + colstat[p, 0:1, at])
        for b in range(start, stop):
            at = slice(b * blk, (b + 1) * blk)
            s = weight[:, (b - start) * blk : (b - start + 1) * blk]
            y = yslots[place(b)]
            go_ref[:, at] = go_ref[:, at] + jnp.sum(y * y, axis=0, keepdims=True)
            ys = y * s
            high, low = split(ys)
            shigh, slow = split(jnp.broadcast_to(s, (8, blk)))
            left[:, at] = jnp.concatenate([high, low, shigh, slow], axis=0).astype(bf16)
            left8[:, at] = to_f8(jnp.concatenate([ys, jnp.broadcast_to(s, (32, blk))], axis=0) * (PT_SCALE * 2.0**LIFT))

    def reload(b, rs):
        k = place(b)
        for r in range(rs.start, rs.stop, 32):
            part = slice(r, r + 32)
            for c in range(rows // chunk):
                at = slice(c * chunk, (c + 1) * chunk)
                keep(table[k, part, at], b % 4, part, at)

    height = 2 * width + 16
    start, stop = parts[-1]
    whole = slice(0, blk)
    reload(0, whole)
    reload(1, whole)
    for part in range(len(parts) - 1):
        weigh(part)
        for b in range(*parts[part], 2):
            rs = slice(b % 4 * blk, (b % 4 + 2) * blk)
            at = slice(b * blk, (b + 2) * blk)
            for c in range(4):
                to = slice(c * (rows // 4), (c + 1) * (rows // 4))
                main = jnp.dot(left[:, at], ehi[rs, to], preferred_element_type=f32)
                rest = jnp.dot(left8[:, at], elo[rs, to], preferred_element_type=f32)
                if b:
                    main = main + acc[0:height, to]
                    rest = rest + acc[height:, to]
                acc[0:height, to] = main
                acc[height:, to] = rest
                reload(b + 2 + c // 2, slice(c % 2 * (blk // 2), (c % 2 + 1) * (blk // 2)))
    for b in range(start + 2, stop):
        reload(b, whole)
    weigh(len(parts) - 1)

    def push(k):
        at = lanes(tgt_peer(k, -1))
        to, kept = slice(start * blk, stop * blk), slice(start % 4 * blk, (start % 4 + stop - start) * blk)
        main = acc[0:height, at] + jnp.dot(left[:, to], ehi[kept, at], preferred_element_type=f32)
        rest = acc[height:, at] + jnp.dot(left8[:, to], elo[kept, at], preferred_element_type=f32)
        rest = rest * (1.0 / (PT_SCALE * 2.0**LIFT))
        moved = main[0:width] + main[width : 2 * width] + rest[0:width]
        mass = main[2 * width : 2 * width + 1] + main[2 * width + 8 : 2 * width + 9] + rest[width : width + 1]
        return 2.0 * (xall[:, at] * mass - moved)

    for k in range(1, nt):
        gsend[k] = push(k)
        if comm:
            gs_copy(k).start()
    grad = push(0)

    mine = lanes(p)
    srow[1:2, 0:blk] = srow[0:1, mine]
    weight = srow[1:2, 0:blk]
    moved = pulled[p] * jnp.exp2(weight + colstat[p, 0:1, mine])
    for k in range(1, ns):
        owner = src_peer(k, -1)
        if comm:
            gt_arrival(k).wait_recv()
        moved = moved + gtrecv[owner] * jnp.exp2(weight + colstat[owner, 0:1, mine])
    gt_ref[...] = 2.0 * (tgt_ref[...] * jnp.exp2(LOG2E * lb_ref[:, mine]) - moved)
    for k in range(1, nt):
        if comm:
            gs_copy(k).wait_recv()
        grad = grad + gsrecv[k]
    gs_ref[...] = grad

    for k in tsteps:
        x_copy(k, q, tgt_peer(k, 1)).wait_send()
        r_copy(k, q, tgt_peer(k, 1)).wait_send()
        gs_copy(k).wait_send()
    for k in ssteps:
        y_copy(k).wait_send()
        for part in range(len(parts)):
            c_copy(part, k, p, src_peer(k, 1)).wait_send()
        gt_arrival(k).wait_send()


def call(ns, ny, nt, nc, comm, width, blk):
    rows, cols = nt * blk, ns * blk
    vmem = pl.BlockSpec(memory_space=pltpu.VMEM)
    dma = pltpu.SemaphoreType.DMA
    scratch = [
        ((width, rows), f32), ((ns, width, blk), f32), ((4 * width, rows), bf16), ((cols, 2 * LANES), bf16),
        ((rows, 2 * LANES), bf16), ((rows, LANES), f8), ((2, blk, LANES), f32), ((ns, blk, rows), f32),
        ((8, rows), f32), ((8, rows), f32), ((8, rows), f32), ((3, blk, LANES), f32),
        ((nt, 2, rows), f32), ((ns, 2, cols), f32), ((8, cols), f32),
        ((4 * blk, rows), bf16), ((4 * blk, rows), f8), ((ns, width, blk), f32),
        ((2 * width + 16, cols), bf16), ((width + 32, cols), f8), ((3 * width + 48, rows), f32),
        ((nt, width, blk), f32), ((nt, width, blk), f32), ((ns, width, blk), f32),
    ]
    waits = len(column_parts(ns)) * ns
    sems = [nt, nt, ns, ns, nt, nt, waits, waits, nt, nt, ns, ns]
    params = dict(vmem_limit_bytes=60 * 2**20, has_side_effects=True)
    if comm:
        params["collective_id"] = 0
    return pl.pallas_call(
        functools.partial(kernel, ns, ny, nt, nc, comm),
        out_shape=[
            jax.ShapeDtypeStruct((1, rows), f32),
            jax.ShapeDtypeStruct((1, cols), f32),
            jax.ShapeDtypeStruct((width, blk), f32),
            jax.ShapeDtypeStruct((width, blk), f32),
        ],
        in_specs=[vmem] * 5,
        out_specs=[vmem] * 4,
        scratch_shapes=[pltpu.VMEM(*s) for s in scratch] + [dma((n,)) for n in sems],
        compiler_params=pltpu.CompilerParams(**params),
        name="sinkhorn",
    )


def solution(mesh):
    ns, nt = mesh.shape["src"], mesh.shape["tgt"]
    ny = 4 if ns % 4 == 0 else 1
    nc = 2 if nt % 2 == 0 else 1

    def per_device(src_points, tgt_points, log_a, log_b, g_init):
        width, blk = src_points.shape
        run = call(ns, ny, nt, nc, True, width, blk)
        f, g, grad_src, grad_tgt = run(
            src_points, tgt_points, log_a.reshape(1, -1), log_b.reshape(1, -1), g_init.reshape(1, -1)
        )
        return f.reshape(-1), g.reshape(-1), grad_src, grad_tgt

    in_specs = (P(None, ("src", "tgt")), P(None, ("tgt", "src")), P("src"), P("tgt"), P("tgt"))
    out_specs = (P("src"), P("tgt"), P(None, ("src", "tgt")), P(None, ("tgt", "src")))
    return jax.shard_map(per_device, mesh=mesh, in_specs=in_specs, out_specs=out_specs, check_vma=False)
```

```python
import functools

import jax
import jax.numpy as jnp
from jax import lax
from jax.experimental import pallas as pl
from jax.experimental.pallas import tpu as pltpu
from jax.sharding import PartitionSpec as P

epsilon = 0.5
LOG2E = 1.4426950408889634
LN2 = 0.6931471805599453
SCALE = LOG2E / epsilon
LIFT = 17.0
PT_SCALE = 2.0**4
F8_MAX = 448.0
MESH = pl.DeviceIdType.MESH
f32, bf16, f8 = jnp.float32, jnp.bfloat16, jnp.float8_e4m3fn
LANES = 128


def split(value):
    high = value.astype(bf16).astype(f32)
    return high, value - high


def to_f8(value):
    return jnp.clip(value, -F8_MAX, F8_MAX).astype(f8)


def wide(column, times):
    return jnp.concatenate([column] * times, axis=1)


def column_parts(ns):
    cuts = [0, 6, 12, 16] if ns == 16 else [0, ns // 2, ns]
    return list(zip(cuts[:-1], cuts[1:]))


def kernel(
    ns, ny, nt, nc, comm,
    src_ref, tgt_ref, la_ref, lb_ref, g_ref,
    f_ref, go_ref, gs_ref, gt_ref,
    xall, yslots, xs, yt, w, w8, bcol, sbuf, mrun, lrun, arow, mcol, rowstat, colstat, srow,
    ehi, elo, pulled, left, left8, gsend, gsrecv, gtrecv,
    sx, rx, sy, ry, sr, rr, sc, rc, sgs, rgs, sgt, rgt,
):
    blk = src_ref.shape[1]
    width = src_ref.shape[0]
    rows, cols = nt * blk, ns * blk
    parts = column_parts(ns)
    if comm:
        p, q = lax.axis_index("src"), lax.axis_index("tgt")
    else:
        p, q = jnp.int32(0), jnp.int32(0)

    def shifted(at, step, count, minor, sign):
        major = count // minor
        a = lax.rem(at // minor + sign * (step // minor) + major, major)
        b = lax.rem(lax.rem(at, minor) + sign * lax.rem(step, minor) + minor, minor)
        return a * minor + b

    def src_peer(step, sign):
        return shifted(p, jnp.int32(step), ns, ny, sign)

    def tgt_peer(step, sign):
        return shifted(q, jnp.int32(step), nt, nc, sign)

    def lanes(owner):
        return pl.ds(pl.multiple_of(owner * blk, blk), blk)

    def remote(source, target, send, recv, device):
        return pltpu.make_async_remote_copy(
            src_ref=source, dst_ref=target, send_sem=send, recv_sem=recv, device_id=device, device_id_type=MESH
        )

    tsteps = range(1, nt) if comm else ()
    ssteps = range(1, ns) if comm else ()
    near = [d for d in (1, ny - 1, 2) if d < ny]
    near_z = [d for d in near if d < ns // ny]


    nz, nx = ns // ny, nt // nc

    def x_copy(k):
        dx, dc = k // nc, k % nc
        if dc == 0 or dx == 0:
            return remote(src_ref, xall.at[:, lanes(q)], sx.at[k], rx.at[k], (p, tgt_peer(k, 1)))
        at = lanes(tgt_peer(dx * nc, -1))
        return remote(xall.at[:, at], xall.at[:, at], sx.at[k], rx.at[k], (p, tgt_peer(dc, 1)))

    def y_copy(k, h):
        dz, dy = k // ny, k % ny
        at, sem = pl.ds(h * (width // 2), width // 2), h * ns + k
        if dz == 0 or dy == 0:
            source, to = tgt_ref.at[at, :], src_peer(k, 1)
        elif h == 0:
            source, to = yslots.at[dz * ny, at, :], src_peer(dy, 1)
        else:
            source, to = yslots.at[dy, at, :], src_peer(dz * ny, 1)
        return remote(source, yslots.at[k, at, :], sy.at[sem], ry.at[sem], (to, q))

    def r_copy(k, owner, to):
        return remote(rowstat.at[q], rowstat.at[owner], sr.at[k], rr.at[k], (p, to))

    def c_copy(part, k, owner, to):
        at = slice(parts[part][0] * blk, parts[part][1] * blk)
        sem = part * ns + k
        return remote(colstat.at[p, :, at], colstat.at[owner, :, at], sc.at[sem], rc.at[sem], (to, q))

    major = ns // ny
    back_z = [lax.rem(t - p // ny + major, major) for t in range(major)]
    back_y = [lax.rem(t - lax.rem(p, ny) + ny, ny) for t in range(ny)]
    block_z = [lax.rem(p // ny - t + major, major) for t in range(major)]
    block_y = [lax.rem(lax.rem(p, ny) - t + ny, ny) for t in range(ny)]

    def place(j, k):
        return back_z[(j // ny + k // ny) % major] * ny + back_y[(j % ny + k % ny) % ny]

    def gs_copy(k):
        return remote(gsend.at[k], gsrecv.at[k], sgs.at[k], rgs.at[k], (p, tgt_peer(k, -1)))

    def gt_copy(k):
        return remote(pulled.at[k], gtrecv.at[k], sgt.at[k], rgt.at[k], (src_peer(k, -1), q))

    if comm:
        barrier = pltpu.get_barrier_semaphore()
        for k in tsteps:
            pl.semaphore_signal(barrier, inc=1, device_id=(p, tgt_peer(k, 1)), device_id_type=MESH)
        for k in ssteps:
            pl.semaphore_signal(barrier, inc=1, device_id=(src_peer(k, 1), q), device_id_type=MESH)
        pl.semaphore_wait(barrier, nt - 1 + ns - 1)

    if comm:
        for k in [dx * nc for dx in (1, 3, 2) if dx < nx] + list(range(1, nc)):
            x_copy(k).start()
        for dz in near_z:
            y_copy(dz * ny, 0).start()
        for dy in near:
            y_copy(dy, 1).start()
        for dz in near_z:
            y_copy(dz * ny, 1).start()
        for dy in near:
            y_copy(dy, 0).start()
    xall[:, lanes(q)] = src_ref[...]
    yslots[0] = tgt_ref[...]

    def prepare_targets(k, slot):
        y = yslots[k]
        scaled = y * (2.0 * SCALE)
        parts = jnp.concatenate(split(scaled), axis=0).T.astype(bf16)
        at = pl.ds(pl.multiple_of(k * blk, blk), blk)
        yt[at, 0:LANES] = parts
        yt[at, LANES : 2 * LANES] = parts
        bias = SCALE * (g_ref[:, lanes(src_peer(k, -1))] - jnp.sum(y * y, axis=0, keepdims=True))
        bcol[slot] = jnp.broadcast_to(bias, (LANES, blk)).T

    def prepare_sources(j):
        at = pl.ds(j * blk, blk)
        x = xall[:, at]
        high, low = split(x)
        xs[0:width, at] = high.astype(bf16)
        xs[width : 2 * width, at] = high.astype(bf16)
        xs[2 * width : 3 * width, at] = low.astype(bf16)
        xs[3 * width : 4 * width, at] = low.astype(bf16)
        w[at, 0:LANES] = jnp.concatenate([high, low], axis=0).T.astype(bf16)
        w[at, LANES : 2 * LANES] = jnp.ones((blk, LANES), bf16)
        parts = jnp.concatenate([x * PT_SCALE, jnp.ones_like(x)], axis=0).T
        w8[at, :] = to_f8(parts)

    chunk = min(512, rows)

    def scores(k, slot, c):
        at = slice(k * blk, (k + 1) * blk) if isinstance(k, int) else lanes(k)
        to = slice(c * chunk, (c + 1) * chunk)
        sbuf[slot, :, to] = jnp.dot(yt[at, :], xs[:, to], preferred_element_type=f32)

    def wait_y(k):
        if comm and near_z:

            @pl.when(jnp.logical_and(k // ny > 0, lax.rem(k, ny) > 0))
            def _():
                for h in range(2):
                    at, sem = pl.ds(h * (width // 2), width // 2), h * ns + k
                    remote(
                        tgt_ref.at[at, :], yslots.at[k, at, :], sy.at[sem], ry.at[sem], (src_peer(k, 1), q)
                    ).wait_recv()

    prepare_targets(0, 0)
    if comm:
        for k in [dx * nc for dx in (1, 3, 2) if dx < nx]:
            x_copy(k).wait_recv()
            for dc in range(1, nc):
                x_copy(k + dc).start()
        for dz, dy in zip(near_z + [0] * (len(near) - len(near_z)), near):
            if dz:
                y_copy(dz * ny, 0).wait_recv()
                for to in near:
                    y_copy(dz * ny + to, 0).start()
            y_copy(dy, 1).wait_recv()
            for to in near_z:
                y_copy(to * ny + dy, 1).start()
        for dz in near_z:
            y_copy(dz * ny, 1).wait_recv()
        for dy in near:
            y_copy(dy, 0).wait_recv()
        for dc in range(1, nc):
            for dx in [0] + [d for d in (1, 3, 2) if d < nx]:
                x_copy(dx * nc + dc).wait_recv()
    for j in range(nt):
        prepare_sources(j)

    mrun[...] = jnp.full(mrun.shape, -jnp.inf, f32)
    lrun[...] = jnp.zeros(lrun.shape, f32)
    def row_pass(slot, c):
        if True:
            at = slice(c * chunk, (c + 1) * chunk)
            old = mrun[:, at]
            top = old
            for r in range(blk // 8):
                rs = slice(8 * r, 8 * r + 8)
                top = jnp.maximum(top, sbuf[slot, rs, at] + wide(bcol[slot, rs, :], chunk // LANES))
            total = lrun[:, at] * jnp.exp2(old - top)
            for r in range(blk // 8):
                rs = slice(8 * r, 8 * r + 8)
                total = total + jnp.exp2(sbuf[slot, rs, at] + (wide(bcol[slot, rs, :], chunk // LANES) - top))
            mrun[:, at] = top
            lrun[:, at] = total

    steps = range(rows // chunk)

    def row_step(k, slot):
        wait_y(k + 1)
        prepare_targets(k + 1, 1 - slot)
        for c in steps:
            scores(k + 1, 1 - slot, c)
            row_pass(slot, c)

    def row_steps(pair, carry):
        row_step(2 * pair, 0)
        row_step(2 * pair + 1, 1)
        return carry

    for c in steps:
        scores(0, 0, c)
    lax.fori_loop(0, ns // 2 - 1, row_steps, 0)
    row_step(jnp.int32(ns - 2), 0)
    for c in steps:
        row_pass(1, c)

    top = jnp.max(mrun[...], axis=0, keepdims=True)
    rowstat[q, 0:1, :] = top
    rowstat[q, 1:2, :] = jnp.sum(lrun[...] * jnp.exp2(mrun[...] - top), axis=0, keepdims=True)
    for k in tsteps:
        r_copy(k, q, tgt_peer(k, 1)).start()
    for c in steps:
        scores(0, 0, c)
    for k in tsteps:
        r_copy(k, tgt_peer(k, -1), tgt_peer(k, 1)).wait_recv()
    top = rowstat[0, 0:1, :]
    for j in range(1, nt):
        top = jnp.maximum(top, rowstat[j, 0:1, :])
    total = jnp.zeros_like(top)
    for j in range(nt):
        total = total + rowstat[j, 1:2, :] * jnp.exp2(rowstat[j, 0:1, :] - top)
    lse = top + jnp.log(total) * LOG2E
    arow[...] = jnp.broadcast_to(LOG2E * la_ref[...] - lse, arow.shape)
    x = xall[...]
    f_ref[...] = epsilon * la_ref[...] - (epsilon * LN2) * lse + jnp.sum(x * x, axis=0, keepdims=True)

    quarter = blk // 4

    def tops(slot, piece):
        rs = slice(piece * quarter, (piece + 1) * quarter)
        top = sbuf[slot, rs, 0:LANES] + arow[0:1, 0:LANES]
        for c in range(1, rows // LANES):
            at = slice(c * LANES, (c + 1) * LANES)
            top = jnp.maximum(top, sbuf[slot, rs, at] + arow[0:1, at])
        top = jnp.max(top, axis=1, keepdims=True) - LIFT
        mcol[slot, rs, :] = jnp.broadcast_to(top, (quarter, LANES))

    def expos(k, slot, piece):
        for r in range(piece * quarter, (piece + 1) * quarter, 32):
            rs = slice(r, r + 32)
            to = slice(k * blk + r, k * blk + r + 32)
            for c in steps:
                at = slice(c * chunk, (c + 1) * chunk)
                e = jnp.exp2(sbuf[slot, rs, at] + (arow[0:1, at] - wide(mcol[slot, rs, :], chunk // LANES)))
                high = e.astype(bf16)
                low = (e - high.astype(f32)).astype(f8)
                ehi[to, at] = high
                elo[to, at] = low

    half = rows // 2

    def pull_product(k, piece):
        rs = slice(k * blk, (k + 1) * blk)
        at = slice(piece % 2 * half, (piece % 2 + 1) * half)
        if piece < 2:
            return jnp.dot(ehi[rs, at], w[at, :], preferred_element_type=f32)
        return jnp.dot(elo[rs, at], w8[at, :], preferred_element_type=f32)

    def pull_finish(k, products):
        main = products[0] + products[1]
        rest = (products[2] + products[3]).T
        first = lax.broadcasted_iota(jnp.int32, (blk, LANES), 1) == 0
        sums = main[:, 0:LANES].T
        stats = jnp.where(first, mcol[2], main[:, LANES : 2 * LANES]).T
        pulled[k] = sums[0:width] + sums[width : 2 * width] + rest[0:width] * (1.0 / PT_SCALE)
        at = slice(k * blk, (k + 1) * blk)
        colstat[p, 0:1, at] = stats[0:1, :]
        colstat[p, 1:2, at] = stats[1:2, :] + rest[width : width + 1, :]

    def turn(k, slot, pulls=True, exps=True, finds=True):
        products = []
        if pulls:
            mcol[2] = mcol[1 - slot]
        for piece in range(4):
            if finds and piece < len(steps):
                scores(k + 1, 1 - slot, piece)
            if pulls:
                products.append(pull_product(k - 1, piece))
            if exps:
                expos(k, slot, piece)
        if pulls:
            pull_finish(k - 1, products)
        if finds:
            for piece in range(4):
                tops(1 - slot, piece)

    def send_stats(part):
        for k in ssteps:
            c_copy(part, k, p, src_peer(k, 1)).start()

    def send_pulled(k, carry):
        gt_copy(k).start()
        return carry

    for piece in range(4):
        tops(0, piece)
    sent, part = 1, 0
    for k in range(ns + 1):
        turn(k, k % 2, pulls=k > 0, exps=k < ns, finds=k + 1 < ns)
        if k == parts[part][1]:
            send_stats(part)
            part += 1
            if comm:
                lax.fori_loop(sent, k, send_pulled, 0)
                sent = k

    for part in range(len(parts)):
        for k in ssteps:
            c_copy(part, k, src_peer(k, -1), src_peer(k, 1)).wait_recv()

    def weigh(k):
        owner = lanes(block_z[k // ny] * ny + block_y[k % ny])
        spots = [lanes(place(j, k)) for j in range(ns)]
        tops = [colstat[j, 0:1, spots[j]] for j in range(ns)]
        top = functools.reduce(jnp.maximum, tops)
        total = jnp.zeros_like(top)
        for j in range(ns):
            total = total + colstat[j, 1:2, spots[j]] * jnp.exp2(tops[j] - top)
        lse = top + jnp.log(total) * LOG2E
        y = yslots[k]
        weight = LOG2E * lb_ref[:, owner] - lse
        srow[0:1, owner] = weight
        square = jnp.sum(y * y, axis=0, keepdims=True)
        go_ref[:, owner] = epsilon * lb_ref[:, owner] - (epsilon * LN2) * lse + square
        at = slice(k * blk, (k + 1) * blk)
        s = jnp.exp2(weight + colstat[p, 0:1, at])
        ys = y * s
        high, low = split(ys)
        shigh, slow = split(jnp.broadcast_to(s, (8, blk)))
        left[:, at] = jnp.concatenate([high, low, shigh, slow], axis=0).astype(bf16)
        left8[:, at] = to_f8(jnp.concatenate([ys, jnp.broadcast_to(s, (32, blk))], axis=0) * (PT_SCALE * 2.0**LIFT))

    for k in range(ns):
        weigh(k)

    def push(k):
        at = lanes(tgt_peer(k, -1))
        main = jnp.dot(left[...], ehi[:, at], preferred_element_type=f32)
        rest = jnp.dot(left8[...], elo[:, at], preferred_element_type=f32) * (1.0 / (PT_SCALE * 2.0**LIFT))
        moved = main[0:width] + main[width : 2 * width] + rest[0:width]
        mass = main[2 * width : 2 * width + 1] + main[2 * width + 8 : 2 * width + 9] + rest[width : width + 1]
        return 2.0 * (xall[:, at] * mass - moved)

    def push_step(k, carry):
        gsend[k] = push(k)
        if comm:
            gs_copy(k).start()
        return carry

    lax.fori_loop(1, nt, push_step, 0)
    grad = push(0)

    mine = lanes(p)
    weight = srow[0:1, mine]
    moved = pulled[0] * jnp.exp2(weight + colstat[p, 0:1, 0:blk])
    for k in range(1, ns):
        if comm:
            gt_copy(k).wait_recv()
        moved = moved + gtrecv[k] * jnp.exp2(weight + colstat[src_peer(k, 1), 0:1, k * blk : (k + 1) * blk])
    gt_ref[...] = 2.0 * (tgt_ref[...] * jnp.exp2(LOG2E * lb_ref[:, mine]) - moved)
    for k in range(1, nt):
        if comm:
            gs_copy(k).wait_recv()
        grad = grad + gsrecv[k]
    gs_ref[...] = grad

    for k in tsteps:
        x_copy(k).wait_send()
        r_copy(k, q, tgt_peer(k, 1)).wait_send()
        gs_copy(k).wait_send()
    for k in ssteps:
        for h in range(2):
            y_copy(k, h).wait_send()
        for part in range(len(parts)):
            c_copy(part, k, p, src_peer(k, 1)).wait_send()
        gt_copy(k).wait_send()


def hand_out(*refs):
    for source, target in zip(refs[:4], refs[4:]):
        target[...] = source[...]


def call(ns, ny, nt, nc, comm, width, blk):
    rows, cols = nt * blk, ns * blk
    vmem = pl.BlockSpec(memory_space=pltpu.VMEM)
    dma = pltpu.SemaphoreType.DMA
    scratch = [
        ((width, rows), f32), ((ns, width, blk), f32), ((4 * width, rows), bf16), ((cols, 2 * LANES), bf16),
        ((rows, 2 * LANES), bf16), ((rows, LANES), f8), ((2, blk, LANES), f32), ((2, blk, rows), f32),
        ((8, rows), f32), ((8, rows), f32), ((8, rows), f32), ((3, blk, LANES), f32),
        ((nt, 2, rows), f32), ((ns, 2, cols), f32), ((8, cols), f32),
        ((cols, rows), bf16), ((cols, rows), f8), ((ns, width, blk), f32),
        ((2 * width + 16, cols), bf16), ((width + 32, cols), f8),
        ((nt, width, blk), f32), ((nt, width, blk), f32), ((ns, width, blk), f32),
    ]
    waits = len(column_parts(ns)) * ns
    sems = [nt, nt, 2 * ns, 2 * ns, nt, nt, waits, waits, nt, nt, ns, ns]
    params = dict(vmem_limit_bytes=60 * 2**20, has_side_effects=True)
    if comm:
        params["collective_id"] = 0
    return pl.pallas_call(
        functools.partial(kernel, ns, ny, nt, nc, comm),
        out_shape=[
            jax.ShapeDtypeStruct((1, rows), f32),
            jax.ShapeDtypeStruct((1, cols), f32),
            jax.ShapeDtypeStruct((width, blk), f32),
            jax.ShapeDtypeStruct((width, blk), f32),
        ],
        in_specs=[vmem] * 5,
        out_specs=[vmem] * 4,
        scratch_shapes=[pltpu.VMEM(*s) for s in scratch] + [dma((n,)) for n in sems],
        compiler_params=pltpu.CompilerParams(**params),
        name="sinkhorn",
    )


def solution(mesh):
    ns, nt = mesh.shape["src"], mesh.shape["tgt"]
    ny = 4 if ns % 4 == 0 else 1
    nc = 2 if nt % 2 == 0 else 1

    def per_device(src_points, tgt_points, log_a, log_b, g_init):
        width, blk = src_points.shape
        run = call(ns, ny, nt, nc, True, width, blk)
        f, g, grad_src, grad_tgt = run(
            src_points, tgt_points, log_a.reshape(1, -1), log_b.reshape(1, -1), g_init.reshape(1, -1)
        )
        vmem = pl.BlockSpec(memory_space=pltpu.VMEM)
        outs = (f, g, grad_src, grad_tgt)
        f, g, grad_src, grad_tgt = pl.pallas_call(
            hand_out,
            out_shape=[jax.ShapeDtypeStruct(o.shape, o.dtype) for o in outs],
            in_specs=[vmem] * 4,
            out_specs=[vmem] * 4,
            name="results",
        )(*outs)
        return f.reshape(-1), g.reshape(-1), grad_src, grad_tgt

    in_specs = (P(None, ("src", "tgt")), P(None, ("tgt", "src")), P("src"), P("tgt"), P("tgt"))
    out_specs = (P("src"), P("tgt"), P(None, ("src", "tgt")), P(None, ("tgt", "src")))
    return jax.shard_map(per_device, mesh=mesh, in_specs=in_specs, out_specs=out_specs, check_vma=False)
```

```python
import functools

import jax
import jax.numpy as jnp
from jax import lax
from jax.experimental import pallas as pl
from jax.experimental.pallas import tpu as pltpu
from jax.sharding import PartitionSpec as P

epsilon = 0.5
LOG2E = 1.4426950408889634
LN2 = 0.6931471805599453
SCALE = LOG2E / epsilon
LIFT = 17.0
PT_SCALE = 2.0**4
F8_MAX = 448.0
MESH = pl.DeviceIdType.MESH
f32, bf16, f8 = jnp.float32, jnp.bfloat16, jnp.float8_e4m3fn
LANES = 128


def split(value):
    high = value.astype(bf16).astype(f32)
    return high, value - high


def to_f8(value):
    return jnp.clip(value, -F8_MAX, F8_MAX).astype(f8)


def wide(column, times):
    return jnp.concatenate([column] * times, axis=1)


def column_parts(ns):
    cuts = [0, 6, 12, 16] if ns == 16 else [0, ns // 2, ns]
    return list(zip(cuts[:-1], cuts[1:]))


def kernel(
    ns, ny, nt, nc, comm,
    src_ref, tgt_ref, la_ref, lb_ref, g_ref,
    f_ref, go_ref, gs_ref, gt_ref,
    xall, yslots, xs, yt, w, w8, bcol, sbuf, table, mrun, lrun, arow, mcol, rowstat, colstat, srow,
    ehi, elo, pulled, left, left8, gsend, gsrecv, gtrecv,
    sx, rx, sy, ry, sr, rr, sc, rc, sgs, rgs, sgt, rgt,
):
    blk = src_ref.shape[1]
    width = src_ref.shape[0]
    rows, cols = nt * blk, ns * blk
    parts = column_parts(ns)
    if comm:
        p, q = lax.axis_index("src"), lax.axis_index("tgt")
    else:
        p, q = jnp.int32(0), jnp.int32(0)

    def shifted(at, step, count, minor, sign):
        major = count // minor
        a = lax.rem(at // minor + sign * (step // minor) + major, major)
        b = lax.rem(lax.rem(at, minor) + sign * lax.rem(step, minor) + minor, minor)
        return a * minor + b

    def src_peer(step, sign):
        return shifted(p, jnp.int32(step), ns, ny, sign)

    def tgt_peer(step, sign):
        return shifted(q, jnp.int32(step), nt, nc, sign)

    def lanes(owner):
        return pl.ds(pl.multiple_of(owner * blk, blk), blk)

    def remote(source, target, send, recv, device):
        return pltpu.make_async_remote_copy(
            src_ref=source, dst_ref=target, send_sem=send, recv_sem=recv, device_id=device, device_id_type=MESH
        )

    tsteps = range(1, nt) if comm else ()
    ssteps = range(1, ns) if comm else ()
    near = [d for d in (1, ny - 1, 2) if d < ny]
    near_z = [d for d in near if d < ns // ny]


    nz, nx = ns // ny, nt // nc

    def x_copy(k):
        dx, dc = k // nc, k % nc
        if dc == 0 or dx == 0:
            return remote(src_ref, xall.at[:, lanes(q)], sx.at[k], rx.at[k], (p, tgt_peer(k, 1)))
        at = lanes(tgt_peer(dx * nc, -1))
        return remote(xall.at[:, at], xall.at[:, at], sx.at[k], rx.at[k], (p, tgt_peer(dc, 1)))

    def y_copy(k, h):
        dz, dy = k // ny, k % ny
        at, sem = pl.ds(h * (width // 2), width // 2), h * ns + k
        if dz == 0 or dy == 0:
            source, to = tgt_ref.at[at, :], src_peer(k, 1)
        elif h == 0:
            source, to = yslots.at[dz * ny, at, :], src_peer(dy, 1)
        else:
            source, to = yslots.at[dy, at, :], src_peer(dz * ny, 1)
        return remote(source, yslots.at[k, at, :], sy.at[sem], ry.at[sem], (to, q))

    def r_copy(k, owner, to):
        return remote(rowstat.at[q], rowstat.at[owner], sr.at[k], rr.at[k], (p, to))

    def c_copy(part, k, owner, to):
        at = slice(parts[part][0] * blk, parts[part][1] * blk)
        sem = part * ns + k
        return remote(colstat.at[p, :, at], colstat.at[owner, :, at], sc.at[sem], rc.at[sem], (to, q))

    major = ns // ny
    back_z = [lax.rem(t - p // ny + major, major) for t in range(major)]
    back_y = [lax.rem(t - lax.rem(p, ny) + ny, ny) for t in range(ny)]
    block_z = [lax.rem(p // ny - t + major, major) for t in range(major)]
    block_y = [lax.rem(lax.rem(p, ny) - t + ny, ny) for t in range(ny)]

    def place(j, k):
        return back_z[(j // ny + k // ny) % major] * ny + back_y[(j % ny + k % ny) % ny]

    def gs_copy(k):
        return remote(gsend.at[k], gsrecv.at[k], sgs.at[k], rgs.at[k], (p, tgt_peer(k, -1)))

    def gt_copy(k):
        return remote(pulled.at[k], gtrecv.at[k], sgt.at[k], rgt.at[k], (src_peer(k, -1), q))

    if comm:
        barrier = pltpu.get_barrier_semaphore()
        for k in tsteps:
            pl.semaphore_signal(barrier, inc=1, device_id=(p, tgt_peer(k, 1)), device_id_type=MESH)
        for k in ssteps:
            pl.semaphore_signal(barrier, inc=1, device_id=(src_peer(k, 1), q), device_id_type=MESH)
        pl.semaphore_wait(barrier, nt - 1 + ns - 1)

    if comm:
        for k in [dx * nc for dx in (1, 3, 2) if dx < nx] + list(range(1, nc)):
            x_copy(k).start()
        for dz in near_z:
            y_copy(dz * ny, 0).start()
        for dy in near:
            y_copy(dy, 1).start()
        for dz in near_z:
            y_copy(dz * ny, 1).start()
        for dy in near:
            y_copy(dy, 0).start()
    xall[:, lanes(q)] = src_ref[...]
    yslots[0] = tgt_ref[...]

    def prepare_targets(k, slot):
        y = yslots[k]
        scaled = y * (2.0 * SCALE)
        parts = jnp.concatenate(split(scaled), axis=0).T.astype(bf16)
        at = pl.ds(pl.multiple_of(k * blk, blk), blk)
        yt[at, 0:LANES] = parts
        yt[at, LANES : 2 * LANES] = parts
        bias = SCALE * (g_ref[:, lanes(src_peer(k, -1))] - jnp.sum(y * y, axis=0, keepdims=True))
        bcol[slot] = jnp.broadcast_to(bias, (LANES, blk)).T

    def prepare_sources(j):
        at = pl.ds(j * blk, blk)
        x = xall[:, at]
        high, low = split(x)
        xs[0:width, at] = high.astype(bf16)
        xs[width : 2 * width, at] = high.astype(bf16)
        xs[2 * width : 3 * width, at] = low.astype(bf16)
        xs[3 * width : 4 * width, at] = low.astype(bf16)
        w[at, 0:LANES] = jnp.concatenate([high, low], axis=0).T.astype(bf16)
        w[at, LANES : 2 * LANES] = jnp.ones((blk, LANES), bf16)
        parts = jnp.concatenate([x * PT_SCALE, jnp.ones_like(x)], axis=0).T
        w8[at, :] = to_f8(parts)

    chunk = min(512, rows)

    kept = 1 + 2 * (ns // 8)

    def scores(k, slot, c, keep=False):
        at = slice(k * blk, (k + 1) * blk) if isinstance(k, int) else lanes(k)
        to = slice(c * chunk, (c + 1) * chunk)
        value = jnp.dot(yt[at, :], xs[:, to], preferred_element_type=f32)
        sbuf[slot, :, to] = value
        if keep:
            table[k, :, to] = value

    def held(k, slot):
        return table.at[k] if k < kept else sbuf.at[slot]

    def wait_y(k):
        if comm and near_z:

            @pl.when(jnp.logical_and(k // ny > 0, lax.rem(k, ny) > 0))
            def _():
                for h in range(2):
                    at, sem = pl.ds(h * (width // 2), width // 2), h * ns + k
                    remote(
                        tgt_ref.at[at, :], yslots.at[k, at, :], sy.at[sem], ry.at[sem], (src_peer(k, 1), q)
                    ).wait_recv()

    prepare_targets(0, 0)
    if comm:
        for k in [dx * nc for dx in (1, 3, 2) if dx < nx]:
            x_copy(k).wait_recv()
            for dc in range(1, nc):
                x_copy(k + dc).start()
        for dz, dy in zip(near_z + [0] * (len(near) - len(near_z)), near):
            if dz:
                y_copy(dz * ny, 0).wait_recv()
                for to in near:
                    y_copy(dz * ny + to, 0).start()
            y_copy(dy, 1).wait_recv()
            for to in near_z:
                y_copy(to * ny + dy, 1).start()
        for dz in near_z:
            y_copy(dz * ny, 1).wait_recv()
        for dy in near:
            y_copy(dy, 0).wait_recv()
        for dc in range(1, nc):
            for dx in [0] + [d for d in (1, 3, 2) if d < nx]:
                x_copy(dx * nc + dc).wait_recv()
    for j in range(nt):
        prepare_sources(j)

    mrun[...] = jnp.full(mrun.shape, -jnp.inf, f32)
    lrun[...] = jnp.zeros(lrun.shape, f32)
    def row_pass(slot, c):
        if True:
            at = slice(c * chunk, (c + 1) * chunk)
            old = mrun[:, at]
            top = old
            for r in range(blk // 8):
                rs = slice(8 * r, 8 * r + 8)
                top = jnp.maximum(top, sbuf[slot, rs, at] + wide(bcol[slot, rs, :], chunk // LANES))
            total = lrun[:, at] * jnp.exp2(old - top)
            for r in range(blk // 8):
                rs = slice(8 * r, 8 * r + 8)
                total = total + jnp.exp2(sbuf[slot, rs, at] + (wide(bcol[slot, rs, :], chunk // LANES) - top))
            mrun[:, at] = top
            lrun[:, at] = total

    steps = range(rows // chunk)

    def row_step(k, slot, keep):
        wait_y(k + 1)
        prepare_targets(k + 1, 1 - slot)
        for c in steps:
            scores(k + 1, 1 - slot, c, keep)
            row_pass(slot, c)

    def row_steps(keep, pair, carry):
        row_step(2 * pair, 0, keep)
        row_step(2 * pair + 1, 1, keep)
        return carry

    for c in steps:
        scores(0, 0, c, True)
    lax.fori_loop(0, kept // 2, functools.partial(row_steps, True), 0)
    lax.fori_loop(kept // 2, ns // 2 - 1, functools.partial(row_steps, False), 0)
    row_step(jnp.int32(ns - 2), 0, False)
    for c in steps:
        row_pass(1, c)

    top = jnp.max(mrun[...], axis=0, keepdims=True)
    rowstat[q, 0:1, :] = top
    rowstat[q, 1:2, :] = jnp.sum(lrun[...] * jnp.exp2(mrun[...] - top), axis=0, keepdims=True)
    for k in tsteps:
        r_copy(k, q, tgt_peer(k, 1)).start()
    for k in tsteps:
        r_copy(k, tgt_peer(k, -1), tgt_peer(k, 1)).wait_recv()
    top = rowstat[0, 0:1, :]
    for j in range(1, nt):
        top = jnp.maximum(top, rowstat[j, 0:1, :])
    total = jnp.zeros_like(top)
    for j in range(nt):
        total = total + rowstat[j, 1:2, :] * jnp.exp2(rowstat[j, 0:1, :] - top)
    lse = top + jnp.log(total) * LOG2E
    arow[...] = jnp.broadcast_to(LOG2E * la_ref[...] - lse, arow.shape)
    x = xall[...]
    f_ref[...] = epsilon * la_ref[...] - (epsilon * LN2) * lse + jnp.sum(x * x, axis=0, keepdims=True)

    quarter = blk // 4

    def tops(k, slot, piece):
        source = held(k, slot)
        rs = slice(piece * quarter, (piece + 1) * quarter)
        top = source[rs, 0:LANES] + arow[0:1, 0:LANES]
        for c in range(1, rows // LANES):
            at = slice(c * LANES, (c + 1) * LANES)
            top = jnp.maximum(top, source[rs, at] + arow[0:1, at])
        top = jnp.max(top, axis=1, keepdims=True) - LIFT
        mcol[slot, rs, :] = jnp.broadcast_to(top, (quarter, LANES))

    def expos(k, slot, piece):
        source = held(k, slot)
        for r in range(piece * quarter, (piece + 1) * quarter, 32):
            rs = slice(r, r + 32)
            to = slice(k * blk + r, k * blk + r + 32)
            for c in steps:
                at = slice(c * chunk, (c + 1) * chunk)
                e = jnp.exp2(source[rs, at] + (arow[0:1, at] - wide(mcol[slot, rs, :], chunk // LANES)))
                high = e.astype(bf16)
                low = (e - high.astype(f32)).astype(f8)
                ehi[to, at] = high
                elo[to, at] = low

    half = rows // 2

    def pull_product(k, piece):
        rs = slice(k * blk, (k + 1) * blk)
        at = slice(piece % 2 * half, (piece % 2 + 1) * half)
        if piece < 2:
            return jnp.dot(ehi[rs, at], w[at, :], preferred_element_type=f32)
        return jnp.dot(elo[rs, at], w8[at, :], preferred_element_type=f32)

    def pull_finish(k, products):
        main = products[0] + products[1]
        rest = (products[2] + products[3]).T
        first = lax.broadcasted_iota(jnp.int32, (blk, LANES), 1) == 0
        sums = main[:, 0:LANES].T
        stats = jnp.where(first, mcol[2], main[:, LANES : 2 * LANES]).T
        pulled[k] = sums[0:width] + sums[width : 2 * width] + rest[0:width] * (1.0 / PT_SCALE)
        at = slice(k * blk, (k + 1) * blk)
        colstat[p, 0:1, at] = stats[0:1, :]
        colstat[p, 1:2, at] = stats[1:2, :] + rest[width : width + 1, :]

    def turn(k, slot, pulls=True, exps=True, finds=True):
        products = []
        if pulls:
            mcol[2] = mcol[1 - slot]
        for piece in range(4):
            if finds and k + 1 >= kept and piece < len(steps):
                scores(k + 1, 1 - slot, piece)
            if pulls:
                products.append(pull_product(k - 1, piece))
            if exps:
                expos(k, slot, piece)
        if pulls:
            pull_finish(k - 1, products)
        if finds:
            for piece in range(4):
                tops(k + 1, 1 - slot, piece)

    def send_stats(part):
        for k in ssteps:
            c_copy(part, k, p, src_peer(k, 1)).start()

    def send_pulled(k, carry):
        gt_copy(k).start()
        return carry

    for piece in range(4):
        tops(0, 0, piece)
    sent, part = 1, 0
    for k in range(ns + 1):
        turn(k, k % 2, pulls=k > 0, exps=k < ns, finds=k + 1 < ns)
        if k == parts[part][1]:
            send_stats(part)
            part += 1
            if comm and part == len(parts):
                lax.fori_loop(sent, k, send_pulled, 0)

    for part in range(len(parts)):
        for k in ssteps:
            c_copy(part, k, src_peer(k, -1), src_peer(k, 1)).wait_recv()

    def weigh(k):
        owner = lanes(block_z[k // ny] * ny + block_y[k % ny])
        spots = [lanes(place(j, k)) for j in range(ns)]
        tops = [colstat[j, 0:1, spots[j]] for j in range(ns)]
        top = functools.reduce(jnp.maximum, tops)
        total = jnp.zeros_like(top)
        for j in range(ns):
            total = total + colstat[j, 1:2, spots[j]] * jnp.exp2(tops[j] - top)
        lse = top + jnp.log(total) * LOG2E
        y = yslots[k]
        weight = LOG2E * lb_ref[:, owner] - lse
        srow[0:1, owner] = weight
        square = jnp.sum(y * y, axis=0, keepdims=True)
        go_ref[:, owner] = epsilon * lb_ref[:, owner] - (epsilon * LN2) * lse + square
        at = slice(k * blk, (k + 1) * blk)
        s = jnp.exp2(weight + colstat[p, 0:1, at])
        ys = y * s
        high, low = split(ys)
        shigh, slow = split(jnp.broadcast_to(s, (8, blk)))
        left[:, at] = jnp.concatenate([high, low, shigh, slow], axis=0).astype(bf16)
        left8[:, at] = to_f8(jnp.concatenate([ys, jnp.broadcast_to(s, (32, blk))], axis=0) * (PT_SCALE * 2.0**LIFT))

    for k in range(ns):
        weigh(k)

    def push(k):
        at = lanes(tgt_peer(k, -1))
        main = jnp.dot(left[...], ehi[:, at], preferred_element_type=f32)
        rest = jnp.dot(left8[...], elo[:, at], preferred_element_type=f32) * (1.0 / (PT_SCALE * 2.0**LIFT))
        moved = main[0:width] + main[width : 2 * width] + rest[0:width]
        mass = main[2 * width : 2 * width + 1] + main[2 * width + 8 : 2 * width + 9] + rest[width : width + 1]
        return 2.0 * (xall[:, at] * mass - moved)

    def push_step(step, carry):
        k = nt - step
        gsend[k] = push(k)
        if comm:
            gs_copy(k).start()
        return carry

    lax.fori_loop(1, nt, push_step, 0)
    grad = push(0)

    mine = lanes(p)
    weight = srow[0:1, mine]
    moved = pulled[0] * jnp.exp2(weight + colstat[p, 0:1, 0:blk])
    for k in range(1, ns):
        if comm:
            gt_copy(k).wait_recv()
        moved = moved + gtrecv[k] * jnp.exp2(weight + colstat[src_peer(k, 1), 0:1, k * blk : (k + 1) * blk])
    gt_ref[...] = 2.0 * (tgt_ref[...] * jnp.exp2(LOG2E * lb_ref[:, mine]) - moved)
    for k in range(1, nt):
        if comm:
            gs_copy(k).wait_recv()
        grad = grad + gsrecv[k]
    gs_ref[...] = grad

    for k in tsteps:
        x_copy(k).wait_send()
        r_copy(k, q, tgt_peer(k, 1)).wait_send()
        gs_copy(k).wait_send()
    for k in ssteps:
        for h in range(2):
            y_copy(k, h).wait_send()
        for part in range(len(parts)):
            c_copy(part, k, p, src_peer(k, 1)).wait_send()
        gt_copy(k).wait_send()


def hand_out(*refs):
    for source, target in zip(refs[:4], refs[4:]):
        target[...] = source[...]


def call(ns, ny, nt, nc, comm, width, blk):
    rows, cols = nt * blk, ns * blk
    vmem = pl.BlockSpec(memory_space=pltpu.VMEM)
    dma = pltpu.SemaphoreType.DMA
    scratch = [
        ((width, rows), f32), ((ns, width, blk), f32), ((4 * width, rows), bf16), ((cols, 2 * LANES), bf16),
        ((rows, 2 * LANES), bf16), ((rows, LANES), f8), ((2, blk, LANES), f32), ((2, blk, rows), f32), ((1 + 2 * (ns // 8), blk, rows), f32),
        ((8, rows), f32), ((8, rows), f32), ((8, rows), f32), ((3, blk, LANES), f32),
        ((nt, 2, rows), f32), ((ns, 2, cols), f32), ((8, cols), f32),
        ((cols, rows), bf16), ((cols, rows), f8), ((ns, width, blk), f32),
        ((2 * width + 16, cols), bf16), ((width + 32, cols), f8),
        ((nt, width, blk), f32), ((nt, width, blk), f32), ((ns, width, blk), f32),
    ]
    waits = len(column_parts(ns)) * ns
    sems = [nt, nt, 2 * ns, 2 * ns, nt, nt, waits, waits, nt, nt, ns, ns]
    params = dict(vmem_limit_bytes=62 * 2**20, has_side_effects=True)
    if comm:
        params["collective_id"] = 0
    return pl.pallas_call(
        functools.partial(kernel, ns, ny, nt, nc, comm),
        out_shape=[
            jax.ShapeDtypeStruct((1, rows), f32),
            jax.ShapeDtypeStruct((1, cols), f32),
            jax.ShapeDtypeStruct((width, blk), f32),
            jax.ShapeDtypeStruct((width, blk), f32),
        ],
        in_specs=[vmem] * 5,
        out_specs=[vmem] * 4,
        scratch_shapes=[pltpu.VMEM(*s) for s in scratch] + [dma((n,)) for n in sems],
        compiler_params=pltpu.CompilerParams(**params),
        name="sinkhorn",
    )


def solution(mesh):
    ns, nt = mesh.shape["src"], mesh.shape["tgt"]
    ny = 4 if ns % 4 == 0 else 1
    nc = 2 if nt % 2 == 0 else 1

    def per_device(src_points, tgt_points, log_a, log_b, g_init):
        width, blk = src_points.shape
        run = call(ns, ny, nt, nc, True, width, blk)
        f, g, grad_src, grad_tgt = run(
            src_points, tgt_points, log_a.reshape(1, -1), log_b.reshape(1, -1), g_init.reshape(1, -1)
        )
        vmem = pl.BlockSpec(memory_space=pltpu.VMEM)
        outs = (f, g, grad_src, grad_tgt)
        f, g, grad_src, grad_tgt = pl.pallas_call(
            hand_out,
            out_shape=[jax.ShapeDtypeStruct(o.shape, o.dtype) for o in outs],
            in_specs=[vmem] * 4,
            out_specs=[vmem] * 4,
            name="results",
        )(*outs)
        return f.reshape(-1), g.reshape(-1), grad_src, grad_tgt

    in_specs = (P(None, ("src", "tgt")), P(None, ("tgt", "src")), P("src"), P("tgt"), P("tgt"))
    out_specs = (P("src"), P("tgt"), P(None, ("src", "tgt")), P(None, ("tgt", "src")))
    return jax.shard_map(per_device, mesh=mesh, in_specs=in_specs, out_specs=out_specs, check_vma=False)
```
